32 devices in a mesh: row: 8 (over y, x, core), col: 4 (over z).
Axes of the slice: x: 2, y: 2, z: 4, core: 2. Of those that a mesh axis runs over, the one named last changes fastest.
Arguments:
- inputs: bfloat16 [512, 6144], P('row', 'col'), may hold values from -6 to 6
- cotangent: bfloat16 [512, 6144], P('row', 'col'), may hold values from -6 to 6
- w_in: bfloat16 [6144, 12288], P('col', 'row'), may hold values from -0.078125 to 0.078125
- w_out: bfloat16 [12288, 6144], P('row', 'col'), may hold values from -0.0546875 to 0.0546875
Outputs:
- grad_inputs: bfloat16 [512, 6144], P('row', 'col')
- grad_w_in: bfloat16 [6144, 12288], P('col', 'row')
- grad_w_out: bfloat16 [12288, 6144], P('row', 'col')
The draws below stay inside these ranges and needn't reach their ends.
All inputs are finite; a program needn't handle non-finite values.
Results may differ from the reference program's by a relative error of at most 0.017.
Values may be sent and summed in bfloat16 or wider, within the bound.
A program may use at most 128 MiB of HBM per device.

```python
import math
import jax
import jax.numpy as jnp
from jax import lax

D = 6144
FF = 12288
TOKENS = 512
N_COL = 4


def spiked(values, rng, source, target, blocks, factor):
    def block_of(dim):
        return (jnp.arange(values.shape[dim]) // (values.shape[dim] // blocks)).reshape((-1,) + (1,) * (values.ndim - 1 - dim))

    first = jax.random.permutation(rng, blocks)[block_of(target)]
    far = (block_of(target) + blocks // 2) % blocks
    return jnp.where((block_of(source) == first) | (block_of(source) == far), factor * values, values)


def shard_levels(own_key, dims, shards, smallest, largest):
    gain = 1.0
    for dim, shards_of in shards:
        draws = jax.random.uniform(jax.random.fold_in(jax.random.fold_in(own_key, 6), dim), (shards_of,), jnp.float32, smallest / len(shards), largest / len(shards))
        gain = gain * jnp.repeat(jnp.exp(draws), dims[dim] // shards_of).reshape((-1,) + (1,) * (len(dims) - 1 - dim))
    return gain


def gaussian(stream_key, dims, scale, most, split=(), kind=jnp.bfloat16):
    loudness = shard_levels(stream_key, dims, split, -0.22, 0.18) if split else 1.0
    entries = jax.random.normal(stream_key, dims, jnp.float32) * scale * loudness
    return jnp.minimum(jnp.maximum(entries, -most), most).astype(kind)


def noise_with(key, extent, scale, limit, split, heavy, dtype=jnp.bfloat16):
    result = scale * jax.random.normal(key, extent, jnp.float32)
    if split:
        result = result * shard_levels(key, extent, split, -0.22, 0.18)
    return jnp.clip(spiked(result, jax.random.fold_in(key, 3), *heavy), -limit, limit).astype(dtype)


def setup_inputs(seed: int = 0) -> dict:
    key_list = jax.random.split(jax.random.key(seed), 5)
    return {
        "inputs": noise_with(key_list[0], (TOKENS, D), 1.0, 6.0, ((0, 8), (1, 4)), (1, 0, 8, 2.0)),
        "cotangent": gaussian(key_list[1], (TOKENS, D), 1.0, 6.0, ((0, 8), (1, 4))),
        "w_in": gaussian(key_list[2], (D, FF), D ** -0.5, 0.078125, ((0, 4), (1, 8))),
        "w_out": gaussian(key_list[3], (FF, D), FF ** -0.5, 0.0546875, ((0, 8), (1, 4))),
    }


cubic_coef = 0.044715
tanh_scale = math.sqrt(2.0 / math.pi)

def block_sum(left, right_cols):
    width = D // N_COL
    total = jnp.zeros((left.shape[0], right_cols.shape[1]), jnp.float32)
    for block in range(N_COL):
        lhs = left[:, block * width:(block + 1) * width]
        rhs = right_cols[block * width:(block + 1) * width, :]
        term = jnp.dot(lhs, rhs, preferred_element_type=jnp.float32).astype(jnp.bfloat16)
        term = lax.optimization_barrier(term)
        total = total + term.astype(jnp.float32)
    return total

def activate(pre, back):
    inner = tanh_scale * (pre + cubic_coef * pre * pre * pre)
    tval = jnp.tanh(inner)
    act = (0.5 * pre * (1.0 + tval)).astype(jnp.bfloat16)
    deriv = 0.5 * (1.0 + tval) + 0.5 * pre * (1.0 - tval * tval) * tanh_scale * (1.0 + 3.0 * cubic_coef * pre * pre)
    slope = (back * deriv).astype(jnp.bfloat16)
    return (act, slope)

def reference(inputs, cotangent, w_in, w_out):
    pre = block_sum(inputs, w_in)
    back = block_sum(cotangent, w_out.T)
    act, slope = activate(pre, back)
    grad_inputs = jnp.dot(slope, w_in.T, preferred_element_type=jnp.float32).astype(jnp.bfloat16)
    grad_w_in = jnp.dot(inputs.T, slope, preferred_element_type=jnp.float32).astype(jnp.bfloat16)
    grad_w_out = jnp.dot(act.T, cotangent, preferred_element_type=jnp.float32).astype(jnp.bfloat16)
    return (grad_inputs, grad_w_in, grad_w_out)
```

```python
import functools
import math

import jax
import jax.numpy as jnp
from jax import lax
from jax.experimental import pallas as pl
from jax.experimental.pallas import tpu as pltpu
from jax.sharding import PartitionSpec as P

cubic_coef = 0.044715
tanh_scale = math.sqrt(2.0 / math.pi)
MESH = pl.DeviceIdType.MESH
NT = (((1,), (1,)), ((), ()))


def activate(pre, back):
    inner = tanh_scale * (pre + cubic_coef * pre * pre * pre)
    tval = jnp.tanh(inner)
    act = (0.5 * pre * (1.0 + tval)).astype(jnp.bfloat16)
    deriv = 0.5 * (1.0 + tval) + 0.5 * pre * (1.0 - tval * tval) * tanh_scale * (
        1.0 + 3.0 * cubic_coef * pre * pre
    )
    slope = (back * deriv).astype(jnp.bfloat16)
    return (act, slope)


def tile_of(width):
    for tile in (512, 384, 256, 128):
        if width % tile == 0:
            return tile
    return width


def kernel(
    rows, cols, own, in_ref, cot_ref, win_hbm, wout_hbm,
    gi_ref, whole_out, res_out,
    win, wout, whole, part, arrived, res, gpart, grecv,
    w_sem, ag_send, ag_recv, red_send, red_recv, bc_send, bc_recv, gi_send, gi_recv, out_sem,
):
    me = lax.axis_index("row")
    z = lax.axis_index("col")
    panel = 2 * own
    panels = rows // 2
    chip = me // 2
    feat = whole.shape[2]
    hidden = part.shape[2]
    last = cols - 1

    load_in = pltpu.make_async_copy(win_hbm, win, w_sem.at[0])
    load_out = pltpu.make_async_copy(wout_hbm, wout, w_sem.at[1])
    load_in.start()
    load_out.start()

    barrier = pltpu.get_barrier_semaphore()

    def greet(i, carry):
        other = lax.rem(me + i, rows)
        pl.semaphore_signal(barrier, inc=1, device_id={"row": other}, device_id_type=MESH)
        return carry

    lax.fori_loop(1, rows, greet, 0)

    @pl.when(z > 0)
    def _():
        pl.semaphore_signal(barrier, inc=1, device_id={"col": z - 1}, device_id_type=MESH)

    @pl.when(z < last)
    def _():
        pl.semaphore_signal(barrier, inc=1, device_id={"col": z + 1}, device_id_type=MESH)

    def block(row):
        return pl.ds(pl.multiple_of(row * own, own), own)

    whole[0, block(me), :] = in_ref[...]
    whole[1, block(me), :] = cot_ref[...]
    pl.semaphore_wait(barrier, rows - 1 + jnp.where(z > 0, 1, 0) + jnp.where(z < last, 1, 0))

    def gather_copy(src, dst):
        return pltpu.make_async_remote_copy(
            src_ref=whole.at[:, block(src), :],
            dst_ref=whole.at[:, block(src), :],
            send_sem=ag_send.at[dst],
            recv_sem=ag_recv.at[src],
            device_id={"row": dst},
            device_id_type=MESH,
        )

    sibling = me + 1 - 2 * lax.rem(me, 2)
    gather_copy(me, sibling).start()

    def push(j, carry):
        target = lax.rem(chip + panels - j, panels)
        gather_copy(me, 2 * target).start()
        gather_copy(me, 2 * target + 1).start()
        return carry

    lax.fori_loop(1, panels, push, 0)

    def panel_of(step):
        return lax.rem(chip + step, panels)

    def half(k, side):
        return block(2 * k + side)

    def red_copy(k, side, target):
        return pltpu.make_async_remote_copy(
            src_ref=part.at[:, half(k, side), :],
            dst_ref=arrived.at[:, half(k, side), :],
            send_sem=red_send.at[side, k],
            recv_sem=red_recv.at[side, k],
            device_id={"col": target},
            device_id_type=MESH,
        )

    def bc_copy(k, side, target):
        return pltpu.make_async_remote_copy(
            src_ref=res.at[:, half(k, side), :],
            dst_ref=res.at[:, half(k, side), :],
            send_sem=bc_send.at[side, k],
            recv_sem=bc_recv.at[side, k],
            device_id={"col": target},
            device_id_type=MESH,
        )

    def gi_copy(owner, src):
        return pltpu.make_async_remote_copy(
            src_ref=gpart.at[block(owner), :],
            dst_ref=grecv.at[src],
            send_sem=gi_send.at[owner],
            recv_sem=gi_recv.at[src],
            device_id={"row": owner},
            device_id_type=MESH,
        )

    place = (z, last - z)
    onward = (1, -1)
    lag = jnp.maximum(z, last - z)

    def forward(step):
        k = panel_of(step)

        @pl.when(step == 0)
        def _():
            gather_copy(sibling, sibling).wait_recv()
            load_in.wait()
            load_out.wait()

        @pl.when(step > 0)
        def _():
            gather_copy(2 * k, sibling).wait_recv()
            gather_copy(2 * k + 1, sibling).wait_recv()

        these = pl.ds(pl.multiple_of(k * panel, panel), panel)
        tile = tile_of(hidden)

        def one(c, carry):
            lanes = pl.ds(pl.multiple_of(c * tile, tile), tile)
            part[0, these, lanes] = jnp.dot(
                whole[0, these, :], win[:, lanes], preferred_element_type=jnp.float32
            ).astype(jnp.bfloat16)
            part[1, these, lanes] = lax.dot_general(
                whole[1, these, :], wout[lanes, :], NT, preferred_element_type=jnp.float32
            ).astype(jnp.bfloat16)
            return carry

        lax.fori_loop(0, hidden // tile, one, 0)

    def reduce_half(step, side):
        k = panel_of(step)
        p = place[side]

        @pl.when(p > 0)
        def _():
            red_copy(k, side, z).wait_recv()

        def summed(which, lines):
            return part[which, lines, :].astype(jnp.float32) + arrived[which, lines, :].astype(jnp.float32)

        def piece(i):
            return pl.ds(pl.multiple_of((2 * k + side) * own + i * 16, 16), 16)

        @pl.when(jnp.logical_and(p > 0, p < last))
        def _():
            def add(i, carry):
                lines = piece(i)
                part[0, lines, :] = summed(0, lines).astype(jnp.bfloat16)
                part[1, lines, :] = summed(1, lines).astype(jnp.bfloat16)
                return carry

            lax.fori_loop(0, own // 16, add, 0)

        @pl.when(p < last)
        def _():
            red_copy(k, side, z + onward[side]).start()

        @pl.when(p == last)
        def _():
            def finish(i, carry):
                lines = piece(i)
                act, slope = activate(summed(0, lines), summed(1, lines))
                res[0, lines, :] = act
                res[1, lines, :] = slope
                return carry

            lax.fori_loop(0, own // 16, finish, 0)
            bc_copy(k, side, z - onward[side]).start()

    def spread_half(step, side):
        k = panel_of(step)
        p = place[side]
        bc_copy(k, side, z).wait_recv()

        @pl.when(p > 0)
        def _():
            bc_copy(k, side, z - onward[side]).start()

    def backward(step):
        k = panel_of(step)
        these = pl.ds(pl.multiple_of(k * panel, panel), panel)
        tile = tile_of(feat)

        def one(c, carry):
            lanes = pl.ds(pl.multiple_of(c * tile, tile), tile)
            gpart[these, lanes] = lax.dot_general(
                res[1, these, :], win[lanes, :], NT, preferred_element_type=jnp.float32
            ).astype(jnp.bfloat16)
            return carry

        lax.fori_loop(0, feat // tile, one, 0)
        for side in range(2):
            owner = 2 * k + side

            @pl.when(owner != me)
            def _():
                gi_copy(owner, me).start()

    def tick(t, carry):
        @pl.when(t < panels)
        def _():
            forward(t)

        back_step = t - 1 - last - lag

        @pl.when(jnp.logical_and(back_step >= 0, back_step < panels))
        def _():
            backward(back_step)

        for side in range(2):
            step = t - place[side]

            @pl.when(jnp.logical_and(step >= 0, step < panels))
            def _():
                reduce_half(step, side)

        for side in range(2):
            step = t - last - (last - place[side])

            @pl.when(jnp.logical_and(place[side] < last, jnp.logical_and(step >= 0, step < panels)))
            def _():
                spread_half(step, side)

        return carry

    lax.fori_loop(0, panels + 2 * last + 1, tick, 0)

    out_whole = pltpu.make_async_copy(whole, whole_out, out_sem.at[0])
    out_res = pltpu.make_async_copy(res, res_out, out_sem.at[1])
    out_whole.start()
    out_res.start()

    def arrive(i, carry):
        src = lax.rem(me + i, rows)
        gi_copy(me, src).wait_recv()
        return carry

    lax.fori_loop(1, rows, arrive, 0)
    grecv[me] = gpart[block(me), :]

    def total(i, carry):
        lines = pl.ds(pl.multiple_of(i * 16, 16), 16)
        acc = grecv[0, lines, :].astype(jnp.float32)
        for r in range(1, rows):
            acc = acc + grecv[r, lines, :].astype(jnp.float32)
        gi_ref[lines, :] = acc.astype(jnp.bfloat16)
        return carry

    lax.fori_loop(0, own // 16, total, 0)

    def drain(i, carry):
        other = lax.rem(me + i, rows)
        gather_copy(me, other).wait_send()
        gi_copy(other, me).wait_send()
        return carry

    lax.fori_loop(1, rows, drain, 0)

    def drain_chain(k, carry):
        for side in range(2):
            @pl.when(place[side] < last)
            def _():
                red_copy(k, side, z).wait_send()

            @pl.when(place[side] > 0)
            def _():
                bc_copy(k, side, z).wait_send()

        return carry

    lax.fori_loop(0, panels, drain_chain, 0)
    out_whole.wait()
    out_res.wait()


def on_device(rows, cols, inputs, cotangent, w_in, w_out):
    own, feat = inputs.shape
    hidden = w_in.shape[1]
    tokens = own * rows
    bf16 = jnp.bfloat16
    vmem = pl.BlockSpec(memory_space=pltpu.VMEM)
    anywhere = pl.BlockSpec(memory_space=pl.ANY)
    dma = pltpu.SemaphoreType.DMA
    panels = rows // 2
    grad_inputs, whole, res = pl.pallas_call(
        functools.partial(kernel, rows, cols, own),
        out_shape=(
            jax.ShapeDtypeStruct((own, feat), bf16),
            jax.ShapeDtypeStruct((2, tokens, feat), bf16),
            jax.ShapeDtypeStruct((2, tokens, hidden), bf16),
        ),
        in_specs=[vmem, vmem, anywhere, anywhere],
        out_specs=(vmem, anywhere, anywhere),
        scratch_shapes=[
            pltpu.VMEM((feat, hidden), bf16),
            pltpu.VMEM((hidden, feat), bf16),
            pltpu.VMEM((2, tokens, feat), bf16),
            pltpu.VMEM((2, tokens, hidden), bf16),
            pltpu.VMEM((2, tokens, hidden), bf16),
            pltpu.VMEM((2, tokens, hidden), bf16),
            pltpu.VMEM((tokens, feat), bf16),
            pltpu.VMEM((rows, own, feat), bf16),
            dma((2,)),
            dma((rows,)),
            dma((rows,)),
            dma((2, panels)),
            dma((2, panels)),
            dma((2, panels)),
            dma((2, panels)),
            dma((rows,)),
            dma((rows,)),
            dma((2,)),
        ],
        compiler_params=pltpu.CompilerParams(
            collective_id=0, has_side_effects=True, vmem_limit_bytes=48 * 1024 * 1024
        ),
        name="mlp_backward",
    )(inputs, cotangent, w_in, w_out)
    grad_w_in = lax.dot_general(
        whole[0], res[1], (((0,), (0,)), ((), ())), preferred_element_type=jnp.float32
    ).astype(bf16)
    grad_w_out = lax.dot_general(
        res[0], whole[1], (((0,), (0,)), ((), ())), preferred_element_type=jnp.float32
    ).astype(bf16)
    return (grad_inputs, grad_w_in, grad_w_out)


def solution(mesh):
    return jax.shard_map(
        functools.partial(on_device, mesh.shape["row"], mesh.shape["col"]),
        mesh=mesh,
        in_specs=(P("row", "col"), P("row", "col"), P("col", "row"), P("row", "col")),
        out_specs=(P("row", "col"), P("col", "row"), P("row", "col")),
        check_vma=False,
    )
```

```python
import functools
import math

import jax
import jax.numpy as jnp
from jax import lax
from jax.experimental import pallas as pl
from jax.experimental.pallas import tpu as pltpu
from jax.sharding import PartitionSpec as P

cubic_coef = 0.044715
tanh_scale = math.sqrt(2.0 / math.pi)
MESH = pl.DeviceIdType.MESH
SPLIT = 3
NT = (((1,), (1,)), ((), ()))


def activate(pre, back):
    inner = tanh_scale * (pre + cubic_coef * pre * pre * pre)
    tval = jnp.tanh(inner)
    act = (0.5 * pre * (1.0 + tval)).astype(jnp.bfloat16)
    deriv = 0.5 * (1.0 + tval) + 0.5 * pre * (1.0 - tval * tval) * tanh_scale * (
        1.0 + 3.0 * cubic_coef * pre * pre
    )
    slope = (back * deriv).astype(jnp.bfloat16)
    return (act, slope)


def tile_of(width):
    for tile in (512, 384, 256, 128):
        if width % tile == 0:
            return tile
    return width


def kernel(
    rows, cols, own, split, in_ref, cot_ref, win_hbm, wout_hbm,
    gi_ref, whole_out, res_out,
    win, wout, whole, part, arrived, res, gpart, grecv, gacc,
    w_sem, ag_send, ag_recv, red_send, red_recv, bc_send, bc_recv, gi_send, gi_recv, out_sem,
):
    me = lax.axis_index("row")
    z = lax.axis_index("col")
    panel = 2 * own
    panels = rows // 2
    chip = me // 2
    feat = whole.shape[2]
    hidden = part.shape[2]
    last = cols - 1
    width = hidden // split
    steps = panels * split

    load_in = pltpu.make_async_copy(win_hbm, win, w_sem.at[0])
    load_out = pltpu.make_async_copy(wout_hbm, wout, w_sem.at[1])

    barrier = pltpu.get_barrier_semaphore()

    def greet(i, carry):
        other = lax.rem(me + i, rows)
        pl.semaphore_signal(barrier, inc=1, device_id={"row": other}, device_id_type=MESH)
        return carry

    lax.fori_loop(1, rows, greet, 0)

    @pl.when(z > 0)
    def _():
        pl.semaphore_signal(barrier, inc=1, device_id={"col": z - 1}, device_id_type=MESH)

    @pl.when(z < last)
    def _():
        pl.semaphore_signal(barrier, inc=1, device_id={"col": z + 1}, device_id_type=MESH)

    def block(row):
        return pl.ds(pl.multiple_of(row * own, own), own)

    mine_in = pltpu.make_async_copy(in_ref, whole.at[0, block(me), :], w_sem.at[2])
    mine_cot = pltpu.make_async_copy(cot_ref, whole.at[1, block(me), :], w_sem.at[3])
    mine_in.start()
    mine_cot.start()
    load_in.start()
    load_out.start()
    mine_in.wait()
    mine_cot.wait()
    pl.semaphore_wait(barrier, rows - 1 + jnp.where(z > 0, 1, 0) + jnp.where(z < last, 1, 0))

    def gather_copy(src, dst):
        return pltpu.make_async_remote_copy(
            src_ref=whole.at[:, block(src), :],
            dst_ref=whole.at[:, block(src), :],
            send_sem=ag_send.at[dst],
            recv_sem=ag_recv.at[src],
            device_id={"row": dst},
            device_id_type=MESH,
        )

    sibling = me + 1 - 2 * lax.rem(me, 2)
    gather_copy(me, sibling).start()

    def push(j, carry):
        target = lax.rem(chip + panels - j, panels)
        gather_copy(me, 2 * target).start()
        gather_copy(me, 2 * target + 1).start()
        return carry

    lax.fori_loop(1, panels, push, 0)

    def panel_of(step):
        return lax.rem(chip + step // split, panels)

    def piece_of(step):
        return lax.rem(step, split)

    def lanes_of(h):
        return pl.ds(pl.multiple_of(h * width, width), width)

    def half(k, side):
        return block(2 * k + side)

    def red_copy(k, h, side, target):
        return pltpu.make_async_remote_copy(
            src_ref=part.at[:, half(k, side), lanes_of(h)],
            dst_ref=arrived.at[:, half(k, side), lanes_of(h)],
            send_sem=red_send.at[side, k * split + h],
            recv_sem=red_recv.at[side, k * split + h],
            device_id={"col": target},
            device_id_type=MESH,
        )

    def bc_copy(k, h, side, target):
        return pltpu.make_async_remote_copy(
            src_ref=res.at[:, half(k, side), lanes_of(h)],
            dst_ref=res.at[:, half(k, side), lanes_of(h)],
            send_sem=bc_send.at[side, k * split + h],
            recv_sem=bc_recv.at[side, k * split + h],
            device_id={"col": target},
            device_id_type=MESH,
        )

    def gi_copy(owner, src):
        return pltpu.make_async_remote_copy(
            src_ref=gpart.at[block(owner), :],
            dst_ref=grecv.at[src],
            send_sem=gi_send.at[owner],
            recv_sem=gi_recv.at[src],
            device_id={"row": owner},
            device_id_type=MESH,
        )

    place = (z, last - z)
    onward = (1, -1)
    lag = jnp.maximum(z, last - z)

    def forward(step):
        k = panel_of(step)
        h = piece_of(step)

        @pl.when(step == 0)
        def _():
            gather_copy(sibling, sibling).wait_recv()
            load_in.wait()
            load_out.wait()

        @pl.when(jnp.logical_and(step > 0, h == 0))
        def _():
            gather_copy(2 * k, sibling).wait_recv()
            gather_copy(2 * k + 1, sibling).wait_recv()

        these = pl.ds(pl.multiple_of(k * panel, panel), panel)
        tile = tile_of(width)

        def one(c, carry):
            lanes = pl.ds(pl.multiple_of(h * width + c * tile, tile), tile)
            part[0, these, lanes] = jnp.dot(
                whole[0, these, :], win[:, lanes], preferred_element_type=jnp.float32
            ).astype(jnp.bfloat16)
            part[1, these, lanes] = lax.dot_general(
                whole[1, these, :], wout[lanes, :], NT, preferred_element_type=jnp.float32
            ).astype(jnp.bfloat16)
            return carry

        lax.fori_loop(0, width // tile, one, 0)

    def reduce_half(step, side):
        k = panel_of(step)
        h = piece_of(step)
        lanes = lanes_of(h)
        p = place[side]

        @pl.when(p > 0)
        def _():
            red_copy(k, h, side, z).wait_recv()

        def summed(which, lines):
            return part[which, lines, lanes].astype(jnp.float32) + arrived[which, lines, lanes].astype(jnp.float32)

        def piece(i):
            return pl.ds(pl.multiple_of((2 * k + side) * own + i * 16, 16), 16)

        @pl.when(jnp.logical_and(p > 0, p < last))
        def _():
            def add(i, carry):
                lines = piece(i)
                part[0, lines, lanes] = summed(0, lines).astype(jnp.bfloat16)
                part[1, lines, lanes] = summed(1, lines).astype(jnp.bfloat16)
                return carry

            lax.fori_loop(0, own // 16, add, 0)

        @pl.when(p < last)
        def _():
            red_copy(k, h, side, z + onward[side]).start()

        @pl.when(p == last)
        def _():
            def finish(i, carry):
                lines = piece(i)
                act, slope = activate(summed(0, lines), summed(1, lines))
                res[0, lines, lanes] = act
                res[1, lines, lanes] = slope
                return carry

            lax.fori_loop(0, own // 16, finish, 0)
            bc_copy(k, h, side, z - onward[side]).start()

    def spread_half(step, side):
        k = panel_of(step)
        h = piece_of(step)
        p = place[side]
        bc_copy(k, h, side, z).wait_recv()

        @pl.when(p > 0)
        def _():
            bc_copy(k, h, side, z - onward[side]).start()

    def backward(step):
        k = panel_of(step)
        h = piece_of(step)
        these = pl.ds(pl.multiple_of(k * panel, panel), panel)
        tile = tile_of(feat)

        def one(c, carry):
            lanes = pl.ds(pl.multiple_of(c * tile, tile), tile)
            term = lax.dot_general(
                res[1, these, lanes_of(h)],
                win[lanes, lanes_of(h)],
                NT,
                preferred_element_type=jnp.float32,
            )
            if split > 1:
                @pl.when(h == 0)
                def _():
                    gacc[:, lanes] = term

                @pl.when(h > 0)
                def _():
                    gacc[:, lanes] += term

                @pl.when(h == split - 1)
                def _():
                    gpart[these, lanes] = gacc[:, lanes].astype(jnp.bfloat16)
            else:
                gpart[these, lanes] = term.astype(jnp.bfloat16)
            return carry

        lax.fori_loop(0, feat // tile, one, 0)
        for side in range(2):
            owner = 2 * k + side

            @pl.when(jnp.logical_and(owner != me, h == split - 1))
            def _():
                gi_copy(owner, me).start()

    def tick(t, carry):
        @pl.when(t < steps)
        def _():
            forward(t)

        back_step = t - 1 - last - lag

        @pl.when(jnp.logical_and(back_step >= 0, back_step < steps))
        def _():
            backward(back_step)

        for side in range(2):
            step = t - place[side]

            @pl.when(jnp.logical_and(step >= 0, step < steps))
            def _():
                reduce_half(step, side)

        for side in range(2):
            step = t - last - (last - place[side])

            @pl.when(jnp.logical_and(place[side] < last, jnp.logical_and(step >= 0, step < steps)))
            def _():
                spread_half(step, side)

        return carry

    lax.fori_loop(0, steps + 2 * last + 1, tick, 0)

    out_whole = pltpu.make_async_copy(whole, whole_out, out_sem.at[0])
    out_res = pltpu.make_async_copy(res, res_out, out_sem.at[1])
    out_whole.start()
    out_res.start()

    def arrive(i, carry):
        src = lax.rem(me + i, rows)
        gi_copy(me, src).wait_recv()
        return carry

    lax.fori_loop(1, rows, arrive, 0)
    grecv[me] = gpart[block(me), :]

    def total(i, carry):
        lines = pl.ds(pl.multiple_of(i * 16, 16), 16)
        acc = grecv[0, lines, :].astype(jnp.float32)
        for r in range(1, rows):
            acc = acc + grecv[r, lines, :].astype(jnp.float32)
        gi_ref[lines, :] = acc.astype(jnp.bfloat16)
        return carry

    lax.fori_loop(0, own // 16, total, 0)

    def drain(i, carry):
        other = lax.rem(me + i, rows)
        gather_copy(me, other).wait_send()
        gi_copy(other, me).wait_send()
        return carry

    lax.fori_loop(1, rows, drain, 0)

    def drain_chain(step, carry):
        k = step // split
        h = piece_of(step)
        for side in range(2):
            @pl.when(place[side] < last)
            def _():
                red_copy(k, h, side, z).wait_send()

            @pl.when(place[side] > 0)
            def _():
                bc_copy(k, h, side, z).wait_send()

        return carry

    lax.fori_loop(0, steps, drain_chain, 0)
    out_whole.wait()
    out_res.wait()


def on_device(rows, cols, inputs, cotangent, w_in, w_out):
    own, feat = inputs.shape
    hidden = w_in.shape[1]
    tokens = own * rows
    bf16 = jnp.bfloat16
    vmem = pl.BlockSpec(memory_space=pltpu.VMEM)
    anywhere = pl.BlockSpec(memory_space=pl.ANY)
    dma = pltpu.SemaphoreType.DMA
    split = SPLIT if hidden % (128 * SPLIT) == 0 else 1
    steps = rows // 2 * split
    grad_inputs, whole, res = pl.pallas_call(
        functools.partial(kernel, rows, cols, own, split),
        out_shape=(
            jax.ShapeDtypeStruct((own, feat), bf16),
            jax.ShapeDtypeStruct((2, tokens, feat), bf16),
            jax.ShapeDtypeStruct((2, tokens, hidden), bf16),
        ),
        in_specs=[anywhere] * 4,
        out_specs=(vmem, anywhere, anywhere),
        scratch_shapes=[
            pltpu.VMEM((feat, hidden), bf16),
            pltpu.VMEM((hidden, feat), bf16),
            pltpu.VMEM((2, tokens, feat), bf16),
            pltpu.VMEM((2, tokens, hidden), bf16),
            pltpu.VMEM((2, tokens, hidden), bf16),
            pltpu.VMEM((2, tokens, hidden), bf16),
            pltpu.VMEM((tokens, feat), bf16),
            pltpu.VMEM((rows, own, feat), bf16),
            pltpu.VMEM((2 * own, feat), jnp.float32),
            dma((4,)),
            dma((rows,)),
            dma((rows,)),
            dma((2, steps)),
            dma((2, steps)),
            dma((2, steps)),
            dma((2, steps)),
            dma((rows,)),
            dma((rows,)),
            dma((2,)),
        ],
        compiler_params=pltpu.CompilerParams(
            collective_id=0, has_side_effects=True, vmem_limit_bytes=48 * 1024 * 1024
        ),
        name="mlp_backward",
    )(inputs, cotangent, w_in, w_out)
    grad_w_in = lax.dot_general(
        whole[0], res[1], (((0,), (0,)), ((), ())), preferred_element_type=jnp.float32
    ).astype(bf16)
    grad_w_out = lax.dot_general(
        res[0], whole[1], (((0,), (0,)), ((), ())), preferred_element_type=jnp.float32
    ).astype(bf16)
    return (grad_inputs, grad_w_in, grad_w_out)


def solution(mesh):
    return jax.shard_map(
        functools.partial(on_device, mesh.shape["row"], mesh.shape["col"]),
        mesh=mesh,
        in_specs=(P("row", "col"), P("row", "col"), P("col", "row"), P("row", "col")),
        out_specs=(P("row", "col"), P("col", "row"), P("row", "col")),
        check_vma=False,
    )
```

```python
import functools
import math

import jax
import jax.numpy as jnp
from jax import lax
from jax.experimental import pallas as pl
from jax.experimental.pallas import tpu as pltpu
from jax.sharding import PartitionSpec as P

cubic_coef = 0.044715
tanh_scale = math.sqrt(2.0 / math.pi)
MESH = pl.DeviceIdType.MESH
SPLIT = 6
SKEW = 2
NT = (((1,), (1,)), ((), ()))


def activate(pre, back):
    inner = tanh_scale * (pre + cubic_coef * pre * pre * pre)
    tval = jnp.tanh(inner)
    act = (0.5 * pre * (1.0 + tval)).astype(jnp.bfloat16)
    deriv = 0.5 * (1.0 + tval) + 0.5 * pre * (1.0 - tval * tval) * tanh_scale * (
        1.0 + 3.0 * cubic_coef * pre * pre
    )
    slope = (back * deriv).astype(jnp.bfloat16)
    return (act, slope)


def tile_of(width):
    for tile in (512, 384, 256, 128):
        if width % tile == 0:
            return tile
    return width


def kernel(
    rows, cols, own, split, in_ref, cot_ref, win_hbm, wout_hbm,
    gi_ref, whole_out, res_out,
    win, wout, whole, part, arrived, res, gpart, grecv, gacc,
    w_sem, ag_send, ag_recv, red_send, red_recv, bc_send, bc_recv, gi_send, gi_recv, out_sem,
):
    me = lax.axis_index("row")
    z = lax.axis_index("col")
    panel = 2 * own
    panels = rows // 2
    chip = me // 2
    feat = whole.shape[2]
    hidden = part.shape[2]
    last = cols - 1
    width = hidden // split
    steps = panels * split

    load_in = pltpu.make_async_copy(win_hbm, win, w_sem.at[0])
    load_out = pltpu.make_async_copy(wout_hbm, wout, w_sem.at[1])

    barrier = pltpu.get_barrier_semaphore()

    def greet(i, carry):
        other = lax.rem(me + i, rows)
        pl.semaphore_signal(barrier, inc=1, device_id={"row": other}, device_id_type=MESH)
        return carry

    lax.fori_loop(1, rows, greet, 0)

    @pl.when(z > 0)
    def _():
        pl.semaphore_signal(barrier, inc=1, device_id={"col": z - 1}, device_id_type=MESH)

    @pl.when(z < last)
    def _():
        pl.semaphore_signal(barrier, inc=1, device_id={"col": z + 1}, device_id_type=MESH)

    def block(row):
        return pl.ds(pl.multiple_of(row * own, own), own)

    mine_in = pltpu.make_async_copy(in_ref, whole.at[0, block(me), :], w_sem.at[2])
    mine_cot = pltpu.make_async_copy(cot_ref, whole.at[1, block(me), :], w_sem.at[3])
    mine_in.start()
    mine_cot.start()
    load_in.start()
    load_out.start()
    mine_in.wait()
    mine_cot.wait()
    pl.semaphore_wait(barrier, rows - 1 + jnp.where(z > 0, 1, 0) + jnp.where(z < last, 1, 0))

    def gather_copy(src, dst):
        return pltpu.make_async_remote_copy(
            src_ref=whole.at[:, block(src), :],
            dst_ref=whole.at[:, block(src), :],
            send_sem=ag_send.at[dst],
            recv_sem=ag_recv.at[src],
            device_id={"row": dst},
            device_id_type=MESH,
        )

    sibling = me + 1 - 2 * lax.rem(me, 2)
    gather_copy(me, sibling).start()

    def push(j, carry):
        target = lax.rem(chip + panels - j, panels)
        gather_copy(me, 2 * target).start()
        gather_copy(me, 2 * target + 1).start()
        return carry

    lax.fori_loop(1, panels, push, 0)

    def panel_of(step):
        return lax.rem(chip + step // split, panels)

    def piece_of(step):
        return lax.rem(step, split)

    def lanes_of(h):
        return pl.ds(pl.multiple_of(h * width, width), width)

    def half(k, side):
        return block(2 * k + side)

    def red_copy(k, h, side, target):
        return pltpu.make_async_remote_copy(
            src_ref=part.at[:, half(k, side), lanes_of(h)],
            dst_ref=arrived.at[:, half(k, side), lanes_of(h)],
            send_sem=red_send.at[side, k * split + h],
            recv_sem=red_recv.at[side, k * split + h],
            device_id={"col": target},
            device_id_type=MESH,
        )

    def bc_copy(k, h, side, target):
        return pltpu.make_async_remote_copy(
            src_ref=res.at[:, half(k, side), lanes_of(h)],
            dst_ref=res.at[:, half(k, side), lanes_of(h)],
            send_sem=bc_send.at[side, k * split + h],
            recv_sem=bc_recv.at[side, k * split + h],
            device_id={"col": target},
            device_id_type=MESH,
        )

    def gi_copy(owner, src):
        return pltpu.make_async_remote_copy(
            src_ref=gpart.at[block(owner), :],
            dst_ref=grecv.at[src],
            send_sem=gi_send.at[owner],
            recv_sem=gi_recv.at[src],
            device_id={"row": owner},
            device_id_type=MESH,
        )

    place = (z, last - z)
    onward = (1, -1)
    lag = jnp.maximum(z, last - z)

    def forward(step):
        k = panel_of(step)
        h = piece_of(step)

        @pl.when(step == 0)
        def _():
            gather_copy(sibling, sibling).wait_recv()
            load_in.wait()
            load_out.wait()

        @pl.when(jnp.logical_and(step > 0, h == 0))
        def _():
            gather_copy(2 * k, sibling).wait_recv()
            gather_copy(2 * k + 1, sibling).wait_recv()

        these = pl.ds(pl.multiple_of(k * panel, panel), panel)
        tile = tile_of(width)

        def one(c, carry):
            lanes = pl.ds(pl.multiple_of(h * width + c * tile, tile), tile)
            part[0, these, lanes] = jnp.dot(
                whole[0, these, :], win[:, lanes], preferred_element_type=jnp.float32
            ).astype(jnp.bfloat16)
            part[1, these, lanes] = lax.dot_general(
                whole[1, these, :], wout[lanes, :], NT, preferred_element_type=jnp.float32
            ).astype(jnp.bfloat16)
            return carry

        lax.fori_loop(0, width // tile, one, 0)

    def reduce_half(step, side):
        k = panel_of(step)
        h = piece_of(step)
        lanes = lanes_of(h)
        p = place[side]

        @pl.when(p > 0)
        def _():
            red_copy(k, h, side, z).wait_recv()

        def summed(which, lines):
            return part[which, lines, lanes].astype(jnp.float32) + arrived[which, lines, lanes].astype(jnp.float32)

        def piece(i):
            return pl.ds(pl.multiple_of((2 * k + side) * own + i * 16, 16), 16)

        @pl.when(jnp.logical_and(p > 0, p < last))
        def _():
            def add(i, carry):
                lines = piece(i)
                part[0, lines, lanes] = summed(0, lines).astype(jnp.bfloat16)
                part[1, lines, lanes] = summed(1, lines).astype(jnp.bfloat16)
                return carry

            lax.fori_loop(0, own // 16, add, 0)

        @pl.when(p < last)
        def _():
            red_copy(k, h, side, z + onward[side]).start()

        @pl.when(p == last)
        def _():
            def finish(i, carry):
                lines = piece(i)
                act, slope = activate(summed(0, lines), summed(1, lines))
                res[0, lines, lanes] = act
                res[1, lines, lanes] = slope
                return carry

            lax.fori_loop(0, own // 16, finish, 0)
            bc_copy(k, h, side, z - onward[side]).start()

    def spread_half(step, side):
        k = panel_of(step)
        h = piece_of(step)
        p = place[side]
        bc_copy(k, h, side, z).wait_recv()

        @pl.when(p > 0)
        def _():
            bc_copy(k, h, side, z - onward[side]).start()

    def backward(step):
        k = panel_of(step)
        h = piece_of(step)
        these = pl.ds(pl.multiple_of(k * panel, panel), panel)
        tile = tile_of(feat)

        def one(c, carry):
            lanes = pl.ds(pl.multiple_of(c * tile, tile), tile)
            term = lax.dot_general(
                res[1, these, lanes_of(h)],
                win[lanes, lanes_of(h)],
                NT,
                preferred_element_type=jnp.float32,
            )
            if split > 1:
                @pl.when(h == 0)
                def _():
                    gacc[:, lanes] = term

                @pl.when(h > 0)
                def _():
                    gacc[:, lanes] += term

                @pl.when(h == split - 1)
                def _():
                    gpart[these, lanes] = gacc[:, lanes].astype(jnp.bfloat16)
            else:
                gpart[these, lanes] = term.astype(jnp.bfloat16)
            return carry

        lax.fori_loop(0, feat // tile, one, 0)
        for side in range(2):
            owner = 2 * k + side

            @pl.when(jnp.logical_and(owner != me, h == split - 1))
            def _():
                gi_copy(owner, me).start()

    def tick(t, carry):
        @pl.when(t < steps)
        def _():
            forward(t)

        back_step = t - 1 - SKEW * (last + lag)

        @pl.when(jnp.logical_and(back_step >= 0, back_step < steps))
        def _():
            backward(back_step)

        for side in range(2):
            step = t - SKEW * place[side]

            @pl.when(jnp.logical_and(step >= 0, step < steps))
            def _():
                reduce_half(step, side)

        for side in range(2):
            step = t - SKEW * (2 * last - place[side])

            @pl.when(jnp.logical_and(place[side] < last, jnp.logical_and(step >= 0, step < steps)))
            def _():
                spread_half(step, side)

        return carry

    lax.fori_loop(0, steps + 2 * SKEW * last + 1, tick, 0)

    out_whole = pltpu.make_async_copy(whole, whole_out, out_sem.at[0])
    out_res = pltpu.make_async_copy(res, res_out, out_sem.at[1])
    out_whole.start()
    out_res.start()

    def arrive(i, carry):
        src = lax.rem(me + i, rows)
        gi_copy(me, src).wait_recv()
        return carry

    lax.fori_loop(1, rows, arrive, 0)
    grecv[me] = gpart[block(me), :]

    def total(i, carry):
        lines = pl.ds(pl.multiple_of(i * 16, 16), 16)
        acc = grecv[0, lines, :].astype(jnp.float32)
        for r in range(1, rows):
            acc = acc + grecv[r, lines, :].astype(jnp.float32)
        gi_ref[lines, :] = acc.astype(jnp.bfloat16)
        return carry

    lax.fori_loop(0, own // 16, total, 0)

    def drain(i, carry):
        other = lax.rem(me + i, rows)
        gather_copy(me, other).wait_send()
        gi_copy(other, me).wait_send()
        return carry

    lax.fori_loop(1, rows, drain, 0)

    def drain_chain(step, carry):
        k = step // split
        h = piece_of(step)
        for side in range(2):
            @pl.when(place[side] < last)
            def _():
                red_copy(k, h, side, z).wait_send()

            @pl.when(place[side] > 0)
            def _():
                bc_copy(k, h, side, z).wait_send()

        return carry

    lax.fori_loop(0, steps, drain_chain, 0)
    out_whole.wait()
    out_res.wait()


def on_device(rows, cols, inputs, cotangent, w_in, w_out):
    own, feat = inputs.shape
    hidden = w_in.shape[1]
    tokens = own * rows
    bf16 = jnp.bfloat16
    vmem = pl.BlockSpec(memory_space=pltpu.VMEM)
    anywhere = pl.BlockSpec(memory_space=pl.ANY)
    dma = pltpu.SemaphoreType.DMA
    split = SPLIT if hidden % (128 * SPLIT) == 0 else 1
    steps = rows // 2 * split
    grad_inputs, whole, res = pl.pallas_call(
        functools.partial(kernel, rows, cols, own, split),
        out_shape=(
            jax.ShapeDtypeStruct((own, feat), bf16),
            jax.ShapeDtypeStruct((2, tokens, feat), bf16),
            jax.ShapeDtypeStruct((2, tokens, hidden), bf16),
        ),
        in_specs=[anywhere] * 4,
        out_specs=(vmem, anywhere, anywhere),
        scratch_shapes=[
            pltpu.VMEM((feat, hidden), bf16),
            pltpu.VMEM((hidden, feat), bf16),
            pltpu.VMEM((2, tokens, feat), bf16),
            pltpu.VMEM((2, tokens, hidden), bf16),
            pltpu.VMEM((2, tokens, hidden), bf16),
            pltpu.VMEM((2, tokens, hidden), bf16),
            pltpu.VMEM((tokens, feat), bf16),
            pltpu.VMEM((rows, own, feat), bf16),
            pltpu.VMEM((2 * own, feat), jnp.float32),
            dma((4,)),
            dma((rows,)),
            dma((rows,)),
            dma((2, steps)),
            dma((2, steps)),
            dma((2, steps)),
            dma((2, steps)),
            dma((rows,)),
            dma((rows,)),
            dma((2,)),
        ],
        compiler_params=pltpu.CompilerParams(
            collective_id=0, has_side_effects=True, vmem_limit_bytes=60 * 1024 * 1024
        ),
        name="mlp_backward",
    )(inputs, cotangent, w_in, w_out)
    grad_w_in = lax.dot_general(
        whole[0], res[1], (((0,), (0,)), ((), ())), preferred_element_type=jnp.float32
    ).astype(bf16)
    grad_w_out = lax.dot_general(
        res[0], whole[1], (((0,), (0,)), ((), ())), preferred_element_type=jnp.float32
    ).astype(bf16)
    return (grad_inputs, grad_w_in, grad_w_out)


def solution(mesh):
    return jax.shard_map(
        functools.partial(on_device, mesh.shape["row"], mesh.shape["col"]),
        mesh=mesh,
        in_specs=(P("row", "col"), P("row", "col"), P("col", "row"), P("row", "col")),
        out_specs=(P("row", "col"), P("col", "row"), P("row", "col")),
        check_vma=False,
    )
```

```python
import functools
import math

import jax
import jax.numpy as jnp
from jax import lax
from jax.experimental import pallas as pl
from jax.experimental.pallas import tpu as pltpu
from jax.sharding import PartitionSpec as P

cubic_coef = 0.044715
tanh_scale = math.sqrt(2.0 / math.pi)
MESH = pl.DeviceIdType.MESH
SPLIT = 6
SKEW = 2
NT = (((1,), (1,)), ((), ()))


def activate(pre, back):
    inner = tanh_scale * (pre + cubic_coef * pre * pre * pre)
    tval = jnp.tanh(inner)
    act = (0.5 * pre * (1.0 + tval)).astype(jnp.bfloat16)
    deriv = 0.5 * (1.0 + tval) + 0.5 * pre * (1.0 - tval * tval) * tanh_scale * (
        1.0 + 3.0 * cubic_coef * pre * pre
    )
    slope = (back * deriv).astype(jnp.bfloat16)
    return (act, slope)


def tile_of(width):
    for tile in (512, 384, 256, 128):
        if width % tile == 0:
            return tile
    return width


def kernel(
    rows, cols, own, split, in_ref, cot_ref, win_hbm, wout_hbm,
    gi_ref, whole_out, res_out,
    win, wout, whole, part, arrived, res, gpart, grecv, gacc,
    w_sem, ag_send, ag_recv, red_send, red_recv, bc_send, bc_recv, gi_send, gi_recv, out_sem,
):
    me = lax.axis_index("row")
    z = lax.axis_index("col")
    panel = 2 * own
    panels = rows // 2
    chip = me // 2
    feat = whole.shape[2]
    hidden = part.shape[2]
    last = cols - 1
    width = hidden // split
    steps = panels * split

    load_in = pltpu.make_async_copy(win_hbm, win, w_sem.at[0])
    load_out = pltpu.make_async_copy(wout_hbm, wout, w_sem.at[1])

    barrier = pltpu.get_barrier_semaphore()

    def greet(i, carry):
        other = lax.rem(me + i, rows)
        pl.semaphore_signal(barrier, inc=1, device_id={"row": other}, device_id_type=MESH)
        return carry

    lax.fori_loop(1, rows, greet, 0)

    @pl.when(z > 0)
    def _():
        pl.semaphore_signal(barrier, inc=1, device_id={"col": z - 1}, device_id_type=MESH)

    @pl.when(z < last)
    def _():
        pl.semaphore_signal(barrier, inc=1, device_id={"col": z + 1}, device_id_type=MESH)

    def block(row):
        return pl.ds(pl.multiple_of(row * own, own), own)

    mine_in = pltpu.make_async_copy(in_ref, whole.at[0, block(me), :], w_sem.at[2])
    mine_cot = pltpu.make_async_copy(cot_ref, whole.at[1, block(me), :], w_sem.at[3])
    mine_in.start()
    mine_cot.start()
    load_in.start()
    load_out.start()
    mine_in.wait()
    mine_cot.wait()
    pl.semaphore_wait(barrier, rows - 1 + jnp.where(z > 0, 1, 0) + jnp.where(z < last, 1, 0))

    def gather_copy(src, dst):
        return pltpu.make_async_remote_copy(
            src_ref=whole.at[:, block(src), :],
            dst_ref=whole.at[:, block(src), :],
            send_sem=ag_send.at[dst],
            recv_sem=ag_recv.at[src],
            device_id={"row": dst},
            device_id_type=MESH,
        )

    sibling = me + 1 - 2 * lax.rem(me, 2)
    gather_copy(me, sibling).start()

    def push(j, carry):
        target = lax.rem(chip + panels - j, panels)
        gather_copy(me, 2 * target).start()
        gather_copy(me, 2 * target + 1).start()
        return carry

    lax.fori_loop(1, panels, push, 0)

    def panel_of(step):
        return lax.rem(chip + step // split, panels)

    def piece_of(step):
        return lax.rem(step, split)

    def lanes_of(h):
        return pl.ds(pl.multiple_of(h * width, width), width)

    def half(k, side):
        return block(2 * k + side)

    def red_copy(k, h, side, target):
        return pltpu.make_async_remote_copy(
            src_ref=part.at[:, half(k, side), lanes_of(h)],
            dst_ref=arrived.at[:, half(k, side), lanes_of(h)],
            send_sem=red_send.at[side, k * split + h],
            recv_sem=red_recv.at[side, k * split + h],
            device_id={"col": target},
            device_id_type=MESH,
        )

    def bc_copy(k, h, side, target):
        return pltpu.make_async_remote_copy(
            src_ref=res.at[:, half(k, side), lanes_of(h)],
            dst_ref=res.at[:, half(k, side), lanes_of(h)],
            send_sem=bc_send.at[side, k * split + h],
            recv_sem=bc_recv.at[side, k * split + h],
            device_id={"col": target},
            device_id_type=MESH,
        )

    def gi_copy(owner, src):
        return pltpu.make_async_remote_copy(
            src_ref=gpart.at[block(owner), :],
            dst_ref=grecv.at[src],
            send_sem=gi_send.at[owner],
            recv_sem=gi_recv.at[src],
            device_id={"row": owner},
            device_id_type=MESH,
        )

    place = (z, last - z)
    onward = (1, -1)
    lag = jnp.maximum(z, last - z)

    def forward(step):
        k = panel_of(step)
        h = piece_of(step)

        @pl.when(step == 0)
        def _():
            gather_copy(sibling, sibling).wait_recv()
            load_in.wait()
            load_out.wait()

        @pl.when(jnp.logical_and(step > 0, h == 0))
        def _():
            gather_copy(2 * k, sibling).wait_recv()
            gather_copy(2 * k + 1, sibling).wait_recv()

        these = pl.ds(pl.multiple_of(k * panel, panel), panel)
        tile = tile_of(width)

        def one(c, carry):
            lanes = pl.ds(pl.multiple_of(h * width + c * tile, tile), tile)
            part[0, these, lanes] = jnp.dot(
                whole[0, these, :], win[:, lanes], preferred_element_type=jnp.float32
            ).astype(jnp.bfloat16)
            part[1, these, lanes] = lax.dot_general(
                whole[1, these, :], wout[lanes, :], NT, preferred_element_type=jnp.float32
            ).astype(jnp.bfloat16)
            return carry

        lax.fori_loop(0, width // tile, one, 0)

    def reduce_half(step, side):
        k = panel_of(step)
        h = piece_of(step)
        lanes = lanes_of(h)
        p = place[side]

        @pl.when(p > 0)
        def _():
            red_copy(k, h, side, z).wait_recv()

        def summed(which, lines):
            return part[which, lines, lanes].astype(jnp.float32) + arrived[which, lines, lanes].astype(jnp.float32)

        def piece(i):
            return pl.ds(pl.multiple_of((2 * k + side) * own + i * 16, 16), 16)

        @pl.when(jnp.logical_and(p > 0, p < last))
        def _():
            def add(i, carry):
                lines = piece(i)
                part[0, lines, lanes] = summed(0, lines).astype(jnp.bfloat16)
                part[1, lines, lanes] = summed(1, lines).astype(jnp.bfloat16)
                return carry

            lax.fori_loop(0, own // 16, add, 0)

        @pl.when(p < last)
        def _():
            red_copy(k, h, side, z + onward[side]).start()

        @pl.when(p == last)
        def _():
            def finish(i, carry):
                lines = piece(i)
                act, slope = activate(summed(0, lines), summed(1, lines))
                res[0, lines, lanes] = act
                res[1, lines, lanes] = slope
                return carry

            lax.fori_loop(0, own // 16, finish, 0)
            bc_copy(k, h, side, z - onward[side]).start()

    def spread_half(step, side):
        k = panel_of(step)
        h = piece_of(step)
        p = place[side]
        bc_copy(k, h, side, z).wait_recv()

        @pl.when(p > 0)
        def _():
            bc_copy(k, h, side, z - onward[side]).start()

    def backward(step):
        k = panel_of(step)
        h = piece_of(step)
        these = pl.ds(pl.multiple_of(k * panel, panel), panel)
        tile = tile_of(feat)

        def one(c, carry):
            lanes = pl.ds(pl.multiple_of(c * tile, tile), tile)
            term = lax.dot_general(
                res[1, these, lanes_of(h)],
                win[lanes, lanes_of(h)],
                NT,
                preferred_element_type=jnp.float32,
            )
            if split > 1:
                @pl.when(h == 0)
                def _():
                    gacc[:, lanes] = term

                @pl.when(h > 0)
                def _():
                    gacc[:, lanes] += term

                @pl.when(h == split - 1)
                def _():
                    gpart[these, lanes] = gacc[:, lanes].astype(jnp.bfloat16)
            else:
                gpart[these, lanes] = term.astype(jnp.bfloat16)
            return carry

        lax.fori_loop(0, feat // tile, one, 0)
        for side in range(2):
            owner = 2 * k + side

            @pl.when(jnp.logical_and(owner != me, h == split - 1))
            def _():
                gi_copy(owner, me).start()

    def tick(t, carry):
        @pl.when(t < steps)
        def _():
            forward(t)

        for side in range(2):
            step = t - SKEW * place[side]

            @pl.when(jnp.logical_and(step >= 0, step < steps))
            def _():
                reduce_half(step, side)

        for side in range(2):
            step = t - SKEW * (2 * last - place[side])

            @pl.when(jnp.logical_and(place[side] < last, jnp.logical_and(step >= 0, step < steps)))
            def _():
                spread_half(step, side)

        back_step = t - SKEW * (last + lag)

        @pl.when(jnp.logical_and(back_step >= 0, back_step < steps))
        def _():
            backward(back_step)

        return carry

    lax.fori_loop(0, steps + 2 * SKEW * last, tick, 0)

    out_whole = pltpu.make_async_copy(whole, whole_out, out_sem.at[0])
    out_res = pltpu.make_async_copy(res, res_out, out_sem.at[1])
    out_whole.start()
    out_res.start()

    def arrive(i, carry):
        src = lax.rem(me + i, rows)
        gi_copy(me, src).wait_recv()
        return carry

    lax.fori_loop(1, rows, arrive, 0)
    grecv[me] = gpart[block(me), :]

    def total(i, carry):
        lines = pl.ds(pl.multiple_of(i * 16, 16), 16)
        acc = grecv[0, lines, :].astype(jnp.float32)
        for r in range(1, rows):
            acc = acc + grecv[r, lines, :].astype(jnp.float32)
        gi_ref[lines, :] = acc.astype(jnp.bfloat16)
        return carry

    lax.fori_loop(0, own // 16, total, 0)

    def drain(i, carry):
        other = lax.rem(me + i, rows)
        gather_copy(me, other).wait_send()
        gi_copy(other, me).wait_send()
        return carry

    lax.fori_loop(1, rows, drain, 0)

    def drain_chain(step, carry):
        k = step // split
        h = piece_of(step)
        for side in range(2):
            @pl.when(place[side] < last)
            def _():
                red_copy(k, h, side, z).wait_send()

            @pl.when(place[side] > 0)
            def _():
                bc_copy(k, h, side, z).wait_send()

        return carry

    lax.fori_loop(0, steps, drain_chain, 0)
    out_whole.wait()
    out_res.wait()


def on_device(rows, cols, inputs, cotangent, w_in, w_out):
    own, feat = inputs.shape
    hidden = w_in.shape[1]
    tokens = own * rows
    bf16 = jnp.bfloat16
    vmem = pl.BlockSpec(memory_space=pltpu.VMEM)
    anywhere = pl.BlockSpec(memory_space=pl.ANY)
    dma = pltpu.SemaphoreType.DMA
    split = SPLIT if hidden % (128 * SPLIT) == 0 else 1
    steps = rows // 2 * split
    grad_inputs, whole, res = pl.pallas_call(
        functools.partial(kernel, rows, cols, own, split),
        out_shape=(
            jax.ShapeDtypeStruct((own, feat), bf16),
            jax.ShapeDtypeStruct((2, tokens, feat), bf16),
            jax.ShapeDtypeStruct((2, tokens, hidden), bf16),
        ),
        in_specs=[anywhere] * 4,
        out_specs=(vmem, anywhere, anywhere),
        scratch_shapes=[
            pltpu.VMEM((feat, hidden), bf16),
            pltpu.VMEM((hidden, feat), bf16),
            pltpu.VMEM((2, tokens, feat), bf16),
            pltpu.VMEM((2, tokens, hidden), bf16),
            pltpu.VMEM((2, tokens, hidden), bf16),
            pltpu.VMEM((2, tokens, hidden), bf16),
            pltpu.VMEM((tokens, feat), bf16),
            pltpu.VMEM((rows, own, feat), bf16),
            pltpu.VMEM((2 * own, feat), jnp.float32),
            dma((4,)),
            dma((rows,)),
            dma((rows,)),
            dma((2, steps)),
            dma((2, steps)),
            dma((2, steps)),
            dma((2, steps)),
            dma((rows,)),
            dma((rows,)),
            dma((2,)),
        ],
        compiler_params=pltpu.CompilerParams(
            collective_id=0, has_side_effects=True, vmem_limit_bytes=60 * 1024 * 1024
        ),
        name="mlp_backward",
    )(inputs, cotangent, w_in, w_out)
    grad_w_in = lax.dot_general(
        whole[0], res[1], (((0,), (0,)), ((), ())), preferred_element_type=jnp.float32
    ).astype(bf16)
    grad_w_out = lax.dot_general(
        res[0], whole[1], (((0,), (0,)), ((), ())), preferred_element_type=jnp.float32
    ).astype(bf16)
    return (grad_inputs, grad_w_in, grad_w_out)


def solution(mesh):
    return jax.shard_map(
        functools.partial(on_device, mesh.shape["row"], mesh.shape["col"]),
        mesh=mesh,
        in_specs=(P("row", "col"), P("row", "col"), P("col", "row"), P("row", "col")),
        out_specs=(P("row", "col"), P("col", "row"), P("row", "col")),
        check_vma=False,
    )
```

```python
import functools
import math

import jax
import jax.numpy as jnp
from jax import lax
from jax.experimental import pallas as pl
from jax.experimental.pallas import tpu as pltpu
from jax.sharding import PartitionSpec as P

cubic_coef = 0.044715
tanh_scale = math.sqrt(2.0 / math.pi)
MESH = pl.DeviceIdType.MESH
SPLIT = 6
SKEW = 2
NT = (((1,), (1,)), ((), ()))


def activate(pre, back):
    inner = tanh_scale * (pre + cubic_coef * pre * pre * pre)
    tval = jnp.tanh(inner)
    act = (0.5 * pre * (1.0 + tval)).astype(jnp.bfloat16)
    deriv = 0.5 * (1.0 + tval) + 0.5 * pre * (1.0 - tval * tval) * tanh_scale * (
        1.0 + 3.0 * cubic_coef * pre * pre
    )
    slope = (back * deriv).astype(jnp.bfloat16)
    return (act, slope)


def tile_of(width):
    for tile in (512, 384, 256, 128):
        if width % tile == 0:
            return tile
    return width


def kernel(
    rows, cols, own, split, in_ref, cot_ref, win_hbm, wout_hbm,
    gi_ref, whole_out, res_out,
    win, wout, whole, part, arrived, res, gpart, grecv, gacc,
    w_sem, ag_send, ag_recv, red_send, red_recv, bc_send, bc_recv, gi_send, gi_recv, out_sem,
):
    me = lax.axis_index("row")
    z = lax.axis_index("col")
    panel = 2 * own
    panels = rows // 2
    chip = me // 2
    feat = whole.shape[2]
    hidden = part.shape[2]
    last = cols - 1
    width = hidden // split
    steps = panels * split

    load_in = pltpu.make_async_copy(win_hbm, win, w_sem.at[0])
    load_out = pltpu.make_async_copy(wout_hbm, wout, w_sem.at[1])

    barrier = pltpu.get_barrier_semaphore()

    def greet(i, carry):
        other = lax.rem(me + i, rows)
        pl.semaphore_signal(barrier, inc=1, device_id={"row": other}, device_id_type=MESH)
        return carry

    lax.fori_loop(1, rows, greet, 0)

    @pl.when(z > 0)
    def _():
        pl.semaphore_signal(barrier, inc=1, device_id={"col": z - 1}, device_id_type=MESH)

    @pl.when(z < last)
    def _():
        pl.semaphore_signal(barrier, inc=1, device_id={"col": z + 1}, device_id_type=MESH)

    def block(row):
        return pl.ds(pl.multiple_of(row * own, own), own)

    mine_in = pltpu.make_async_copy(in_ref, whole.at[0, block(me), :], w_sem.at[2])
    mine_cot = pltpu.make_async_copy(cot_ref, whole.at[1, block(me), :], w_sem.at[3])
    mine_in.start()
    mine_cot.start()
    load_in.start()
    load_out.start()
    mine_in.wait()
    mine_cot.wait()
    pl.semaphore_wait(barrier, rows - 1 + jnp.where(z > 0, 1, 0) + jnp.where(z < last, 1, 0))

    def gather_copy(src, dst):
        return pltpu.make_async_remote_copy(
            src_ref=whole.at[:, block(src), :],
            dst_ref=whole.at[:, block(src), :],
            send_sem=ag_send.at[dst],
            recv_sem=ag_recv.at[src],
            device_id={"row": dst},
            device_id_type=MESH,
        )

    sibling = me + 1 - 2 * lax.rem(me, 2)
    gather_copy(me, sibling).start()

    def push(j, carry):
        target = lax.rem(chip + panels - j, panels)
        gather_copy(me, 2 * target).start()
        gather_copy(me, 2 * target + 1).start()
        return carry

    lax.fori_loop(1, panels, push, 0)

    def panel_of(step):
        return lax.rem(chip + step // split, panels)

    def piece_of(step):
        return lax.rem(step, split)

    def lanes_of(h):
        return pl.ds(pl.multiple_of(h * width, width), width)

    def half(k, side):
        return block(2 * k + side)

    def red_copy(k, h, side, target):
        return pltpu.make_async_remote_copy(
            src_ref=part.at[:, half(k, side), lanes_of(h)],
            dst_ref=arrived.at[:, half(k, side), lanes_of(h)],
            send_sem=red_send.at[side, k * split + h],
            recv_sem=red_recv.at[side, k * split + h],
            device_id={"col": target},
            device_id_type=MESH,
        )

    def bc_copy(k, h, side, target):
        return pltpu.make_async_remote_copy(
            src_ref=res.at[:, half(k, side), lanes_of(h)],
            dst_ref=res.at[:, half(k, side), lanes_of(h)],
            send_sem=bc_send.at[side, k * split + h],
            recv_sem=bc_recv.at[side, k * split + h],
            device_id={"col": target},
            device_id_type=MESH,
        )

    def gi_copy(owner, src):
        return pltpu.make_async_remote_copy(
            src_ref=gpart.at[block(owner), :],
            dst_ref=grecv.at[src],
            send_sem=gi_send.at[owner],
            recv_sem=gi_recv.at[src],
            device_id={"row": owner},
            device_id_type=MESH,
        )

    place = (z, last - z)
    onward = (1, -1)
    lag = jnp.maximum(z, last - z)

    def forward(step):
        k = panel_of(step)
        h = piece_of(step)

        @pl.when(step == 0)
        def _():
            gather_copy(sibling, sibling).wait_recv()
            load_in.wait()
            load_out.wait()

        @pl.when(jnp.logical_and(step > 0, h == 0))
        def _():
            gather_copy(2 * k, sibling).wait_recv()
            gather_copy(2 * k + 1, sibling).wait_recv()

        these = pl.ds(pl.multiple_of(k * panel, panel), panel)
        tile = tile_of(width)

        def one(c, carry):
            lanes = pl.ds(pl.multiple_of(h * width + c * tile, tile), tile)
            part[0, these, lanes] = jnp.dot(
                whole[0, these, :], win[:, lanes], preferred_element_type=jnp.float32
            ).astype(jnp.bfloat16)
            part[1, these, lanes] = lax.dot_general(
                whole[1, these, :], wout[lanes, :], NT, preferred_element_type=jnp.float32
            ).astype(jnp.bfloat16)
            return carry

        lax.fori_loop(0, width // tile, one, 0)

    def reduce_half(step, side):
        k = panel_of(step)
        h = piece_of(step)
        lanes = lanes_of(h)
        p = place[side]

        @pl.when(p > 0)
        def _():
            red_copy(k, h, side, z).wait_recv()

        def summed(which, lines):
            return part[which, lines, lanes].astype(jnp.float32) + arrived[which, lines, lanes].astype(jnp.float32)

        def piece(i):
            return pl.ds(pl.multiple_of((2 * k + side) * own + i * 16, 16), 16)

        @pl.when(jnp.logical_and(p > 0, p < last))
        def _():
            def add(i, carry):
                lines = piece(i)
                part[0, lines, lanes] = summed(0, lines).astype(jnp.bfloat16)
                part[1, lines, lanes] = summed(1, lines).astype(jnp.bfloat16)
                return carry

            lax.fori_loop(0, own // 16, add, 0)

        @pl.when(p < last)
        def _():
            red_copy(k, h, side, z + onward[side]).start()

        @pl.when(p == last)
        def _():
            def finish(i, carry):
                lines = piece(i)
                act, slope = activate(summed(0, lines), summed(1, lines))
                res[0, lines, lanes] = act
                res[1, lines, lanes] = slope
                return carry

            lax.fori_loop(0, own // 16, finish, 0)
            bc_copy(k, h, side, z - onward[side]).start()

    def spread_half(step, side):
        k = panel_of(step)
        h = piece_of(step)
        p = place[side]
        bc_copy(k, h, side, z).wait_recv()

        @pl.when(p > 0)
        def _():
            bc_copy(k, h, side, z - onward[side]).start()

    def backward(step):
        k = panel_of(step)
        h = piece_of(step)
        these = pl.ds(pl.multiple_of(k * panel, panel), panel)
        tile = tile_of(feat)

        def one(c, carry):
            lanes = pl.ds(pl.multiple_of(c * tile, tile), tile)
            term = lax.dot_general(
                res[1, these, lanes_of(h)],
                win[lanes, lanes_of(h)],
                NT,
                preferred_element_type=jnp.float32,
            )
            if split > 1:
                @pl.when(h == 0)
                def _():
                    gacc[:, lanes] = term

                @pl.when(h > 0)
                def _():
                    gacc[:, lanes] += term

                @pl.when(h == split - 1)
                def _():
                    gpart[these, lanes] = gacc[:, lanes].astype(jnp.bfloat16)
            else:
                gpart[these, lanes] = term.astype(jnp.bfloat16)
            return carry

        lax.fori_loop(0, feat // tile, one, 0)
        for side in range(2):
            owner = 2 * k + side

            @pl.when(jnp.logical_and(owner != me, h == split - 1))
            def _():
                gi_copy(owner, me).start()

    def tick(t, carry):
        @pl.when(t < steps)
        def _():
            forward(t)

        for side in range(2):
            step = t - SKEW * place[side]

            @pl.when(jnp.logical_and(step >= 0, step < steps))
            def _():
                reduce_half(step, side)

        for side in range(2):
            step = t - SKEW * last - (last - place[side])

            @pl.when(jnp.logical_and(place[side] < last, jnp.logical_and(step >= 0, step < steps)))
            def _():
                spread_half(step, side)

        back_step = t - SKEW * last - lag

        @pl.when(jnp.logical_and(back_step >= 0, back_step < steps))
        def _():
            backward(back_step)

        return carry

    lax.fori_loop(0, steps + SKEW * last + last, tick, 0)

    out_whole = pltpu.make_async_copy(whole, whole_out, out_sem.at[0])
    out_res = pltpu.make_async_copy(res, res_out, out_sem.at[1])
    out_whole.start()
    out_res.start()

    def arrive(i, carry):
        src = lax.rem(me + i, rows)
        gi_copy(me, src).wait_recv()
        return carry

    lax.fori_loop(1, rows, arrive, 0)
    grecv[me] = gpart[block(me), :]

    def total(i, carry):
        lines = pl.ds(pl.multiple_of(i * 16, 16), 16)
        acc = grecv[0, lines, :].astype(jnp.float32)
        for r in range(1, rows):
            acc = acc + grecv[r, lines, :].astype(jnp.float32)
        gi_ref[lines, :] = acc.astype(jnp.bfloat16)
        return carry

    lax.fori_loop(0, own // 16, total, 0)

    def drain(i, carry):
        other = lax.rem(me + i, rows)
        gather_copy(me, other).wait_send()
        gi_copy(other, me).wait_send()
        return carry

    lax.fori_loop(1, rows, drain, 0)

    def drain_chain(step, carry):
        k = step // split
        h = piece_of(step)
        for side in range(2):
            @pl.when(place[side] < last)
            def _():
                red_copy(k, h, side, z).wait_send()

            @pl.when(place[side] > 0)
            def _():
                bc_copy(k, h, side, z).wait_send()

        return carry

    lax.fori_loop(0, steps, drain_chain, 0)
    out_whole.wait()
    out_res.wait()


def on_device(rows, cols, inputs, cotangent, w_in, w_out):
    own, feat = inputs.shape
    hidden = w_in.shape[1]
    tokens = own * rows
    bf16 = jnp.bfloat16
    vmem = pl.BlockSpec(memory_space=pltpu.VMEM)
    anywhere = pl.BlockSpec(memory_space=pl.ANY)
    dma = pltpu.SemaphoreType.DMA
    split = SPLIT if hidden % (128 * SPLIT) == 0 else 1
    steps = rows // 2 * split
    grad_inputs, whole, res = pl.pallas_call(
        functools.partial(kernel, rows, cols, own, split),
        out_shape=(
            jax.ShapeDtypeStruct((own, feat), bf16),
            jax.ShapeDtypeStruct((2, tokens, feat), bf16),
            jax.ShapeDtypeStruct((2, tokens, hidden), bf16),
        ),
        in_specs=[anywhere] * 4,
        out_specs=(vmem, anywhere, anywhere),
        scratch_shapes=[
            pltpu.VMEM((feat, hidden), bf16),
            pltpu.VMEM((hidden, feat), bf16),
            pltpu.VMEM((2, tokens, feat), bf16),
            pltpu.VMEM((2, tokens, hidden), bf16),
            pltpu.VMEM((2, tokens, hidden), bf16),
            pltpu.VMEM((2, tokens, hidden), bf16),
            pltpu.VMEM((tokens, feat), bf16),
            pltpu.VMEM((rows, own, feat), bf16),
            pltpu.VMEM((2 * own, feat), jnp.float32),
            dma((4,)),
            dma((rows,)),
            dma((rows,)),
            dma((2, steps)),
            dma((2, steps)),
            dma((2, steps)),
            dma((2, steps)),
            dma((rows,)),
            dma((rows,)),
            dma((2,)),
        ],
        compiler_params=pltpu.CompilerParams(
            collective_id=0, has_side_effects=True, vmem_limit_bytes=60 * 1024 * 1024
        ),
        name="mlp_backward",
    )(inputs, cotangent, w_in, w_out)
    grad_w_in = lax.dot_general(
        whole[0], res[1], (((0,), (0,)), ((), ())), preferred_element_type=jnp.float32
    ).astype(bf16)
    grad_w_out = lax.dot_general(
        res[0], whole[1], (((0,), (0,)), ((), ())), preferred_element_type=jnp.float32
    ).astype(bf16)
    return (grad_inputs, grad_w_in, grad_w_out)


def solution(mesh):
    return jax.shard_map(
        functools.partial(on_device, mesh.shape["row"], mesh.shape["col"]),
        mesh=mesh,
        in_specs=(P("row", "col"), P("row", "col"), P("col", "row"), P("row", "col")),
        out_specs=(P("row", "col"), P("col", "row"), P("row", "col")),
        check_vma=False,
    )
```
